512 devices in a mesh: row: 16 (over z_lo, x, core), col: 32 (over z_hi, y).
Axes of the slice: x: 4, y: 8, z: 8 (z_hi: 4, z_lo: 2; z = z_hi * 2 + z_lo), core: 2. Of those that a mesh axis runs over, the one named last changes fastest.
Arguments:
- ymatrix: bfloat16 [2048, 8, 128, 128], P(('row', 'col')), may hold values from -0.36 to 1.36
- zmatrix: bfloat16 [2048, 8, 128, 128], P(('row', 'col')), may hold values from -0.36 to 1.36
- pattern: int32 [2048, 8], P(('row', 'col')), may hold values 0 or 1
Outputs:
- y_update: bfloat16 [2048, 8, 128, 128], P(('row', 'col'))
- z_update: bfloat16 [2048, 8, 128, 128], P(('row', 'col'))
The draws below stay inside these ranges and needn't reach their ends.
All inputs are finite; a program needn't handle non-finite values. No bound on the sum of `pattern` on one device may be relied on, other than what follows from the above.
Results may differ from the reference program's by a relative error of at most 0.008.
Values may be sent and summed in bfloat16 or wider, within the bound.
No kernel may reach another device: no remote copies, remote signals or barrier semaphores. Data moves between devices by JAX's collectives and lax.ppermute only.
A program may use at most 64 MiB of HBM per device.

```python
import jax
import jax.numpy as jnp
from jax import lax

BS = 128
W = 8
HB = 4
RB = 4
NB = 2048


def band_matrix(key):
    shape = (NB, W, BS, BS)
    jitter = jnp.clip(jax.random.normal(key, shape, jnp.float32), -4.0, 4.0) * 0.088
    slot_index = lax.broadcasted_iota(jnp.int32, shape, 1)
    row_index = lax.broadcasted_iota(jnp.int32, shape, 2)
    col_index = lax.broadcasted_iota(jnp.int32, shape, 3)
    identity = jnp.where(jnp.logical_and(slot_index == W // 2, row_index == col_index), 1.0, 0.0)
    return (jitter + identity).astype(jnp.float32)


def draw_ymatrix(key, part):
    key = jax.random.fold_in(key, 11)
    return band_matrix(key).astype(jnp.bfloat16)


def draw_zmatrix(key, part):
    key = jax.random.fold_in(key, 23)
    return band_matrix(key).astype(jnp.bfloat16)


def with_ends(drawn, own_key, least, high):
    dims = drawn.shape
    spot = [jax.random.randint(jax.random.fold_in(own_key, axis), (), 0, dims[axis]) for axis in range(len(dims))]
    drawn = drawn.at[tuple(spot)].set(least)
    longest = dims.index(max(dims))
    spot[longest] = (spot[longest] + 1) % dims[longest]
    return drawn.at[tuple(spot)].set(high)


def setup_inputs(seed: int = 0) -> dict:
    splits = jax.random.split(jax.random.key(seed), 4)
    return {
        "ymatrix": draw_ymatrix(jax.random.fold_in(splits[3], 71), 0),
        "zmatrix": draw_zmatrix(jax.random.fold_in(splits[3], 71), 0),
        "pattern": with_ends((jax.random.randint(splits[2], (NB, W), 0, 4) < 3).astype(jnp.int32), jax.random.fold_in(splits[2], 1), 0, 1),
    }


def band_product(left_side, right_side):
    right_ext = jnp.concatenate([right_side[NB - HB:], right_side, right_side[:HB]], axis=0)
    right_pad = jnp.pad(right_ext, ((0, 0), (HB, HB), (0, 0), (0, 0)))

    def one_block(block_index):
        start = (block_index * RB).astype(jnp.int32)
        left_rows = lax.dynamic_slice_in_dim(left_side, start, RB, 0).astype(jnp.float32)
        right_rows = lax.dynamic_slice_in_dim(right_pad, start, RB + 2 * HB, 0).astype(jnp.float32)
        running = jnp.zeros((RB, W, BS, BS), jnp.float32)
        for offset in range(W):
            window = right_rows[offset:offset + RB, W - offset:2 * W - offset]
            running = running + jnp.einsum('rab,rdbc->rdac', left_rows[:, offset], window)
        return running

    blocks = lax.map(one_block, jnp.arange(NB // RB, dtype=jnp.int32))
    return blocks.reshape(NB, W, BS, BS)


def reference(ymatrix, zmatrix, pattern):
    slot_index = lax.broadcasted_iota(jnp.int32, (NB, W), 1)
    kept_mask = jnp.logical_or(pattern == 1, slot_index == HB)[:, :, None, None]
    y_kept = jnp.where(kept_mask, ymatrix, jnp.zeros_like(ymatrix))
    z_kept = jnp.where(kept_mask, zmatrix, jnp.zeros_like(zmatrix))
    identity = jnp.eye(BS, dtype=jnp.float32)
    diagonal_part = jnp.where((slot_index == HB)[:, :, None, None], 1.5 * identity, jnp.float32(0.0))
    t_blocks = jnp.where(kept_mask, diagonal_part - 0.5 * band_product(z_kept, y_kept), jnp.float32(0.0)).astype(jnp.bfloat16)
    y_update = jnp.where(kept_mask, band_product(y_kept, t_blocks), jnp.float32(0.0)).astype(jnp.bfloat16)
    z_update = jnp.where(kept_mask, band_product(t_blocks, z_kept), jnp.float32(0.0)).astype(jnp.bfloat16)
    return y_update, z_update
```

```python
import jax
import jax.numpy as jnp
from jax import lax
from jax.experimental import pallas as pl
from jax.experimental.pallas import tpu as pltpu
from jax.sharding import PartitionSpec as P

AXES = ("row", "col")
B = 128
S = 512
RING = 8
BF = jnp.bfloat16
F32 = jnp.float32

LOWER = [(r, c) for r in range(4) for c in range(r, 4)]
UPPER = [(r, c) for r in range(4) for c in range(r)]
FULL = [(r, c) for r in range(4) for c in range(4)]


def of(name, blocks):
    return [(name, r, c) for r, c in blocks]


R1 = of("yU", UPPER)
L1 = of("yL", LOWER)
R2 = of("yD", FULL) + of("zU", UPPER[:3])
L2 = of("yD", [(r, c) for r in range(3) for c in range(3)])
R3 = of("zD", FULL) + of("zU", UPPER[3:])
L3 = of("zD", [(r, c) for r in range(3) for c in range(4)]) + of("zL", [p for p in LOWER if p[0] < 3])
L2, L3 = L2 + L3[-3:], L3[:-3]
COLUMN = {"L": 0, "D": S, "U": 2 * S}


def slot(part, r, c):
    return c - r + {"L": 0, "D": 4, "U": 8}[part]


def rows(i, n=1):
    return pl.ds(i * B, n * B)


def dot(a, b):
    return jnp.dot(a, b, preferred_element_type=F32)


def unpack(message, ref, into):
    for i, (name, r, c) in enumerate(message):
        target, row, column = into[name]
        target[pl.ds(row + r * B, B), pl.ds(column + c * B, B)] = ref[rows(i), :]


def keep(pattern, part, r, c):
    d = slot(part, r, c)
    return True if d == 4 else pattern[r, d] == 1


def masked(flag, block):
    return block if flag is True else jnp.where(flag, block, jnp.zeros_like(block))


def pack_kernel(pattern, y, z, r1, l1, r2, l2, r3, l3, yw, zw):
    for wide, source in ((yw, y), (zw, z)):
        for r in range(4):
            for d in range(8):
                k = True if d == 4 else pattern[r, d] == 1
                wide[rows(r), rows(r + d)] = masked(k, source[r, d])
            for c in range(12):
                if not r <= c < r + 8:
                    wide[rows(r), rows(c)] = jnp.zeros((B, B), BF)
    for message, ref in ((R1, r1), (L1, l1), (R2, r2), (L2, l2), (R3, r3), (L3, l3)):
        for i, (name, r, c) in enumerate(message):
            wide = yw if name[0] == "y" else zw
            ref[rows(i), :] = wide[rows(r), pl.ds(COLUMN[name[1]] + c * B, B)]
    line = lax.broadcasted_iota(jnp.int32, (16, B), 0)
    for message, ref in ((R1, r1), (L1, l1)):
        tile = jnp.zeros((16, B), F32)
        for i, (name, r, c) in enumerate(message):
            k = keep(pattern, name[1], r, c)
            tile = jnp.where(line == i, 1.0 if k is True else jnp.where(k, 1.0, 0.0), tile)
        ref[pl.ds(len(message) * B, 16), :] = tile.astype(BF)


def middle_kernel(pattern, yw, zw, r1, l1, td, e, l, column, acc, ud):
    column[pl.ds(0, S), :] = jnp.zeros((S, S), BF)
    column[pl.ds(2 * S, S), :] = jnp.zeros((S, S), BF)
    unpack(R1, r1, {"yU": (column, 0, 0)})
    unpack(L1, l1, {"yL": (column, 2 * S, 0)})
    column[pl.ds(S, S), :] = yw[:, pl.ds(S, S)]
    acc[...] = dot(zw[...], column[...])
    eye = jnp.where(
        lax.broadcasted_iota(jnp.int32, (B, B), 0) == lax.broadcasted_iota(jnp.int32, (B, B), 1), 1.5, 0.0
    )
    for r, c in FULL:
        block = -0.5 * acc[rows(r), rows(c)]
        if r == c:
            block = block + eye
        td[rows(r), rows(c)] = masked(keep(pattern, "D", r, c), block).astype(BF)
    acc[...] = dot(column[pl.ds(2 * S, S), :], td[...])
    for i, (r, c) in enumerate(LOWER):
        e[rows(i), :] = acc[rows(r), rows(c)].astype(BF)
    acc[...] = dot(column[pl.ds(0, S), :], td[...])
    for i, (r, c) in enumerate(UPPER):
        l[rows(i), :] = acc[rows(r), rows(c)].astype(BF)


def last_kernel(
    edge, pattern, yw, zw, td, r1, l1, r2, l2, r3, l3, r3b, l3b, e, l, yout, zout, yb, zb, tb, tw, side, acc
):
    for big in (yb, zb):
        big[pl.ds(0, S), :] = jnp.zeros((S, 3 * S), BF)
        big[pl.ds(2 * S, S), :] = jnp.zeros((S, 3 * S), BF)
    yb[pl.ds(S, S), :] = yw[...]
    zb[pl.ds(S, S), :] = zw[...]
    left = {"yD": (yb, 0, 0), "yU": (yb, 0, S), "zD": (zb, 0, 0), "zU": (zb, 0, S)}
    right = {"yL": (yb, 2 * S, S), "yD": (yb, 2 * S, 2 * S), "zL": (zb, 2 * S, S), "zD": (zb, 2 * S, 2 * S)}
    unpack(R1, r1, left)
    unpack(L1, l1, right)
    unpack(R2, r2, left)
    unpack(L2, l2, right)

    @pl.when(edge[0] == 1)
    def _():
        unpack(R3, r3b, left)

    @pl.when(edge[0] == 0)
    def _():
        unpack(R3, r3, left)

    @pl.when(edge[1] == 1)
    def _():
        unpack(L3, l3b, right)

    @pl.when(edge[1] == 0)
    def _():
        unpack(L3, l3, right)

    tw[...] = jnp.zeros((S, 3 * S), BF)
    tw[:, pl.ds(S, S)] = td[...]
    tb[...] = jnp.zeros((3 * S, S), BF)
    tb[pl.ds(S, S), :] = td[...]
    acc[...] = dot(zw[:, : 2 * S], yb[: 2 * S, :S])
    for r, c in LOWER:
        tw[rows(r), rows(c)] = masked(keep(pattern, "L", r, c), -0.5 * acc[rows(r), rows(c)]).astype(BF)
    acc[...] = dot(zw[:, S:], yb[S:, 2 * S :])
    for r, c in UPPER:
        tw[rows(r), pl.ds(2 * S + c * B, B)] = masked(
            keep(pattern, "U", r, c), -0.5 * acc[rows(r), rows(c)]
        ).astype(BF)
    left_mask = r1[pl.ds(len(R1) * B, 16), :].astype(F32)
    right_mask = l1[pl.ds(len(L1) * B, 16), :].astype(F32)
    acc[...] = dot(zb[:S, : 2 * S], yb[: 2 * S, S : 2 * S])
    for i, (r, c) in enumerate(UPPER):
        tb[rows(r), rows(c)] = (-0.5 * acc[rows(r), rows(c)] * left_mask[i : i + 1, :]).astype(BF)
    acc[...] = dot(zb[2 * S :, S:], yb[S:, S : 2 * S])
    for i, (r, c) in enumerate(LOWER):
        if r < 3:
            tb[pl.ds(2 * S + r * B, B), rows(c)] = (
                -0.5 * acc[rows(r), rows(c)] * right_mask[i : i + 1, :]
            ).astype(BF)

    def finish(out, part, blocks, extra=None):
        for i, (r, c) in enumerate(blocks):
            block = acc[rows(r), rows(c)]
            if extra is not None:
                block = block + extra[rows(i), :].astype(F32)
            out[r, slot(part, r, c)] = masked(keep(pattern, part, r, c), block).astype(BF)

    acc[...] = dot(tw[:, : 2 * S], zb[: 2 * S, :S])
    finish(zout, "L", LOWER)
    acc[...] = dot(tw[...], zb[:, S : 2 * S])
    finish(zout, "D", FULL)
    acc[...] = dot(tw[:, S:], zb[S:, 2 * S :])
    finish(zout, "U", UPPER)
    acc[...] = dot(yw[...], tb[...])
    finish(yout, "D", FULL)
    acc[...] = dot(yw[:, S : 2 * S], tw[:, :S])
    finish(yout, "L", LOWER, e)
    acc[...] = dot(yw[:, S : 2 * S], tw[:, 2 * S :])
    finish(yout, "U", UPPER, l)


VMEM = pl.BlockSpec(memory_space=pltpu.VMEM)
SMEM = pl.BlockSpec(memory_space=pltpu.SMEM)


def packed(message, masks=False):
    return jax.ShapeDtypeStruct((len(message) * B + 16 * masks, B), BF)


def call(kernel, outs, ins, scratch, flops, operands):
    outs = tuple(outs)
    moved = sum(v.size * v.dtype.itemsize for v in (*outs, *operands))
    return pl.pallas_call(
        kernel,
        out_shape=outs,
        in_specs=ins,
        out_specs=tuple(VMEM for _ in outs),
        scratch_shapes=scratch,
        compiler_params=pltpu.CompilerParams(vmem_limit_bytes=48 * 2**20),
        cost_estimate=pl.CostEstimate(flops=flops, bytes_accessed=moved, transcendentals=0),
    )(*operands)


def local(ymatrix, zmatrix, pattern):
    count = lax.axis_size("row") * lax.axis_size("col")
    place = lax.axis_index("col") % RING
    chain = [(i, (i + 1) % count) for i in range(count)]
    near = [p for p in chain if p[0] % RING != RING - 1]
    hop_z = [(i, (i + RING) % count) for i in range(count) if i % RING == RING - 1]
    hop_y = [(i, (i - RING + 1) % count) for i in range(count) if i % RING == RING - 1]

    def back(pairs):
        return [(b, a) for a, b in pairs]

    def flip(pairs):
        return [((count - 1 - a), (count - 1 - b)) for a, b in pairs]

    def send(x, pairs):
        return lax.ppermute(x, AXES, pairs)

    wide = jax.ShapeDtypeStruct((S, 3 * S), BF)
    r1, l1, r2, l2, r3, l3, yw, zw = call(
        pack_kernel,
        (packed(R1, True), packed(L1, True), packed(R2), packed(L2), packed(R3), packed(L3), wide, wide),
        [SMEM, VMEM, VMEM],
        [],
        0,
        (pattern, ymatrix, zmatrix),
    )
    r3z = send(r3, hop_z)
    l3z = send(l3, flip(hop_z))
    r1, l1 = send(r1, chain), send(l1, back(chain))
    r2, l2 = send(r2, chain), send(l2, back(chain))
    r3, l3 = send(r3, near), send(l3, back(near))
    r3b, l3b = send(r3z, hop_y), send(l3z, flip(hop_y))
    td, e, l = call(
        middle_kernel,
        (jax.ShapeDtypeStruct((S, S), BF), packed(LOWER), packed(UPPER)),
        [SMEM] + [VMEM] * 4,
        [pltpu.VMEM((3 * S, S), BF), pltpu.VMEM((S, S), F32), pltpu.VMEM((S, S), BF)],
        10 * S**3,
        (pattern, yw, zw, r1, l1),
    )
    e, l = send(e, chain), send(l, back(chain))
    edge = jnp.stack([place == 0, place == RING - 1]).astype(jnp.int32)
    whole = jax.ShapeDtypeStruct(ymatrix.shape, BF)
    return call(
        last_kernel,
        (whole, whole),
        [SMEM, SMEM] + [VMEM] * 13,
        [
            pltpu.VMEM((3 * S, 3 * S), BF),
            pltpu.VMEM((3 * S, 3 * S), BF),
            pltpu.VMEM((3 * S, S), BF),
            pltpu.VMEM((S, 3 * S), BF),
            pltpu.VMEM((S, S), BF),
            pltpu.VMEM((S, S), F32),
        ],
        40 * S**3,
        (edge, pattern, yw, zw, td, r1, l1, r2, l2, r3, l3, r3b, l3b, e, l),
    )


def solution(mesh):
    band = P(AXES, None, None, None)
    return jax.shard_map(
        local,
        mesh=mesh,
        in_specs=(band, band, P(AXES, None)),
        out_specs=(band, band),
        check_vma=False,
    )
```

```python
import jax
import jax.numpy as jnp
from jax import lax
from jax.experimental import pallas as pl
from jax.experimental.pallas import tpu as pltpu
from jax.sharding import PartitionSpec as P

AXES = ("row", "col")
B = 128
S = 512
H = 256
RING = 8
BF = jnp.bfloat16
F32 = jnp.float32

LOWER = [(r, c) for r in range(4) for c in range(r, 4)]
UPPER = [(r, c) for r in range(4) for c in range(r)]
FULL = [(r, c) for r in range(4) for c in range(4)]


def of(name, blocks):
    return [(name, r, c) for r, c in blocks]


R1 = of("yU", UPPER)
L1 = of("yL", LOWER)
L_TOP = [p for p in LOWER if p[0] < 3]
R_REST = of("yD", FULL) + of("zU", UPPER) + of("zD", FULL)
L_REST = of("yD", [(r, c) for r in range(3) for c in range(3)]) + of("zL", L_TOP) + of("zD", FULL[:12])
R2, R3 = R_REST[:18], R_REST[18:]
L2, L3 = L_REST[:13], L_REST[13:]
COLUMN = {"L": 0, "D": S, "U": 2 * S}
QUADS = {
    "L": ((0, 0), (0, 1), (1, 1)),
    "D": ((0, 0), (0, 1), (1, 0), (1, 1)),
    "U": ((0, 0), (1, 0), (1, 1)),
}
BLOCKS = {"L": LOWER, "D": FULL, "U": UPPER}


def slot(part, r, c):
    return c - r + {"L": 0, "D": 4, "U": 8}[part]


def rows(i, n=1):
    return pl.ds(i * B, n * B)


def unpack(message, ref, into):
    for i, (name, r, c) in enumerate(message):
        target, column = into[name]
        target[rows(r), pl.ds(column + c * B, B)] = ref[rows(i), :]


def clear(target, column, blocks):
    for r, c in FULL:
        if (r, c) not in blocks:
            target[rows(r), pl.ds(column + c * B, B)] = jnp.zeros((B, B), target.dtype)


def product(acc, part, *terms):
    for i, n in QUADS[part]:
        total = None
        for (left, lc, lp), (right, rc, rp) in terms:
            ks = [k for k in (0, 1) if (i, k) in QUADS[lp] and (k, n) in QUADS[rp]]
            if not ks:
                continue
            low, size = ks[0] * H, len(ks) * H
            value = jnp.dot(
                left[pl.ds(i * H, H), pl.ds(lc + low, size)],
                right[pl.ds(low, size), pl.ds(rc + n * H, H)],
                preferred_element_type=F32,
            )
            total = value if total is None else total + value
        acc[pl.ds(i * H, H), pl.ds(n * H, H)] = total


def side(ref, part, column=None):
    return ref, COLUMN[part] if column is None else column, part


def keep(pattern, part, r, c):
    d = slot(part, r, c)
    return True if d == 4 else pattern[r, d] == 1


def masked(flag, block):
    return block if flag is True else jnp.where(flag, block, jnp.zeros_like(block))


def pack_kernel(edge, pattern, y, z, r1, l1, r2, l2, r3, l3, zz, yw, zw, yin, zin, sems):
    copies = []
    for i, (source, target) in enumerate(((y, yin), (z, zin))):
        for r in range(4):
            copies.append(pltpu.make_async_copy(source.at[r], target.at[r], sems.at[i * 4 + r]))
            copies[-1].start()
    for copy in copies:
        copy.wait()
    for wide, source in ((yw, yin), (zw, zin)):
        for r in range(4):
            for d in range(8):
                k = True if d == 4 else pattern[r, d] == 1
                wide[rows(r), rows(r + d)] = masked(k, source[r, d])
            for c in range(12):
                if not r <= c < r + 8:
                    wide[rows(r), rows(c)] = jnp.zeros((B, B), BF)

    def fill(message, ref):
        for i, (name, r, c) in enumerate(message):
            wide = yw if name[0] == "y" else zw
            ref[rows(i), :] = wide[rows(r), pl.ds(COLUMN[name[1]] + c * B, B)]

    for message, ref in ((R1, r1), (L1, l1), (R2, r2), (L2, l2), (R3, r3), (L3, l3)):
        fill(message, ref)

    @pl.when(edge[0] == 1)
    def _():
        fill(L3, zz)

    @pl.when(edge[0] == 0)
    def _():
        fill(R3, zz)

    line = lax.broadcasted_iota(jnp.int32, (16, B), 0)
    for message, ref in ((R1, r1), (L1, l1)):
        tile = jnp.zeros((16, B), F32)
        for i, (name, r, c) in enumerate(message):
            k = keep(pattern, name[1], r, c)
            tile = jnp.where(line == i, 1.0 if k is True else jnp.where(k, 1.0, 0.0), tile)
        ref[pl.ds(len(message) * B, 16), :] = tile.astype(BF)


def middle_kernel(pattern, yw, zw, r1, l1, td, e, l, yu, yl, acc):
    clear(yu, 0, UPPER)
    clear(yl, 0, LOWER)
    unpack(R1, r1, {"yU": (yu, 0)})
    unpack(L1, l1, {"yL": (yl, 0)})
    product(
        acc,
        "D",
        (side(zw, "L"), side(yu, "U", 0)),
        (side(zw, "D"), side(yw, "D")),
        (side(zw, "U"), side(yl, "L", 0)),
    )
    eye = jnp.where(
        lax.broadcasted_iota(jnp.int32, (B, B), 0) == lax.broadcasted_iota(jnp.int32, (B, B), 1), 1.5, 0.0
    )
    for r, c in FULL:
        block = -0.5 * acc[rows(r), rows(c)]
        if r == c:
            block = block + eye
        td[rows(r), rows(c)] = masked(keep(pattern, "D", r, c), block).astype(BF)
    for part, left, out in (("L", yl, e), ("U", yu, l)):
        product(acc, part, (side(left, part, 0), side(td, "D", 0)))
        for i, (r, c) in enumerate(BLOCKS[part]):
            out[rows(i), :] = acc[rows(r), rows(c)].astype(BF)


def last_kernel(pattern, yw, zw, td, r1, l1, r2, l2, r3, l3, e, l, yout, zout, *scratch):
    ya, yc, za, zc, tw, tua, tlc, acc, yo, zo, sems = scratch
    for big in (ya, za):
        clear(big, S, UPPER)
    clear(yc, 0, LOWER)
    clear(zc, 0, L_TOP)
    clear(yc, S, [(r, c) for r in range(3) for c in range(3)])
    clear(zc, S, FULL[:12])
    left = {"yD": (ya, 0), "yU": (ya, S), "zD": (za, 0), "zU": (za, S)}
    right = {"yL": (yc, 0), "yD": (yc, S), "zL": (zc, 0), "zD": (zc, S)}
    for message, ref in ((R1, r1), (R2, r2), (R3, r3)):
        unpack(message, ref, left)
    for message, ref in ((L1, l1), (L2, l2), (L3, l3)):
        unpack(message, ref, right)
    clear(tw, COLUMN["L"], LOWER)
    clear(tw, COLUMN["U"], UPPER)
    clear(tua, 0, UPPER)
    clear(tlc, 0, L_TOP)
    product(acc, "L", (side(zw, "L"), side(ya, "D", 0)), (side(zw, "D"), side(yw, "L")))
    for r, c in LOWER:
        tw[rows(r), rows(c)] = masked(keep(pattern, "L", r, c), -0.5 * acc[rows(r), rows(c)]).astype(BF)
    product(acc, "U", (side(zw, "D"), side(yw, "U")), (side(zw, "U"), side(yc, "D", S)))
    for r, c in UPPER:
        tw[rows(r), pl.ds(2 * S + c * B, B)] = masked(
            keep(pattern, "U", r, c), -0.5 * acc[rows(r), rows(c)]
        ).astype(BF)
    left_mask = r1[pl.ds(len(R1) * B, 16), :].astype(F32)
    right_mask = l1[pl.ds(len(L1) * B, 16), :].astype(F32)
    product(acc, "U", (side(za, "D", 0), side(ya, "U", S)), (side(za, "U", S), side(yw, "D")))
    for i, (r, c) in enumerate(UPPER):
        tua[rows(r), rows(c)] = (-0.5 * acc[rows(r), rows(c)] * left_mask[i : i + 1, :]).astype(BF)
    product(acc, "L", (side(zc, "L", 0), side(yw, "D")), (side(zc, "D", S), side(yc, "L", 0)))
    for i, (r, c) in enumerate(LOWER):
        if r < 3:
            tlc[rows(r), rows(c)] = (-0.5 * acc[rows(r), rows(c)] * right_mask[i : i + 1, :]).astype(BF)

    t_l, t_u, t_d = side(tw, "L"), side(tw, "U"), side(td, "D", 0)

    def finish(out, part, *terms, extra=None):
        product(acc, part, *terms)
        for i, (r, c) in enumerate(BLOCKS[part]):
            block = acc[rows(r), rows(c)]
            if extra is not None:
                block = block + extra[rows(i), :].astype(F32)
            out[r, slot(part, r, c)] = masked(keep(pattern, part, r, c), block).astype(BF)

    copies = []

    def write(source, target):
        for r in range(4):
            copies.append(pltpu.make_async_copy(source.at[r], target.at[r], sems.at[len(copies)]))
            copies[-1].start()

    finish(zo, "L", (t_l, side(za, "D", 0)), (t_d, side(zw, "L")))
    finish(zo, "D", (t_l, side(za, "U", S)), (t_d, side(zw, "D")), (t_u, side(zc, "L", 0)))
    finish(zo, "U", (t_d, side(zw, "U")), (t_u, side(zc, "D", S)))
    write(zo, zout)
    finish(
        yo, "D", (side(yw, "L"), side(tua, "U", 0)), (side(yw, "D"), t_d), (side(yw, "U"), side(tlc, "L", 0))
    )
    finish(yo, "L", (side(yw, "D"), t_l), extra=e)
    finish(yo, "U", (side(yw, "D"), t_u), extra=l)
    write(yo, yout)
    for copy in copies:
        copy.wait()


VMEM = pl.BlockSpec(memory_space=pltpu.VMEM)
SMEM = pl.BlockSpec(memory_space=pltpu.SMEM)
ANY = pl.BlockSpec(memory_space=pl.ANY)


def packed(blocks, masks=False):
    return jax.ShapeDtypeStruct((len(blocks) * B + 16 * masks, B), BF)


def call(kernel, outs, out_specs, ins, scratch, flops, operands):
    outs = tuple(outs)
    moved = sum(v.size * v.dtype.itemsize for v in (*outs, *operands))
    return pl.pallas_call(
        kernel,
        out_shape=outs,
        in_specs=ins,
        out_specs=tuple(out_specs),
        scratch_shapes=scratch,
        compiler_params=pltpu.CompilerParams(vmem_limit_bytes=VMEM_LIMIT),
        cost_estimate=pl.CostEstimate(flops=flops, bytes_accessed=moved, transcendentals=0),
    )(*operands)


VMEM_LIMIT = 32 * 2**20


def local(ymatrix, zmatrix, pattern):
    count = lax.axis_size("row") * lax.axis_size("col")
    place = lax.axis_index("col") % RING
    first, last = place == 0, place == RING - 1
    right = [(i, (i + 1) % count) for i in range(count)]
    left = [(b, a) for a, b in right]
    ends = [(i, (i + RING) % count) for i in range(count) if i % RING == RING - 1]
    ends += [((i + RING) % count, i) for i in range(count) if i % RING == 0]
    right_y = [(i, i + 1 if i % RING < RING - 1 else i - RING + 1) for i in range(count)]
    left_y = [(b, a) for a, b in right_y]

    def send(x, pairs):
        return lax.ppermute(x, AXES, pairs)

    wide = jax.ShapeDtypeStruct((S, 3 * S), BF)
    edge = jnp.stack([first, last]).astype(jnp.int32)
    r1, l1, r2, l2, r3, l3, zz, yw, zw = call(
        pack_kernel,
        (packed(R1, True), packed(L1, True)) + tuple(packed(m) for m in (R2, L2, R3, L3, R3)) + (wide, wide),
        [VMEM] * 9,
        [SMEM, SMEM, ANY, ANY],
        [
            pltpu.VMEM(ymatrix.shape, BF),
            pltpu.VMEM(ymatrix.shape, BF),
            pltpu.SemaphoreType.DMA((8,)),
        ],
        0,
        (edge, pattern, ymatrix, zmatrix),
    )
    r1, l1 = send(r1, right), send(l1, left)
    zz = send(zz, ends)
    r2, l2 = send(r2, right), send(l2, left)
    td, e, l = call(
        middle_kernel,
        (jax.ShapeDtypeStruct((S, S), BF), packed(LOWER), packed(UPPER)),
        [VMEM] * 3,
        [SMEM] + [VMEM] * 4,
        [pltpu.VMEM((S, S), BF), pltpu.VMEM((S, S), BF), pltpu.VMEM((S, S), F32)],
        6 * S**3,
        (pattern, yw, zw, r1, l1),
    )
    e, l = send(e, right), send(l, left)
    r3 = send(jnp.where(last, zz, r3), right_y)
    l3 = send(jnp.where(first, zz[: len(L3) * B], l3), left_y)
    whole = jax.ShapeDtypeStruct(ymatrix.shape, BF)
    half = pltpu.VMEM((S, 2 * S), BF)
    return call(
        last_kernel,
        (whole, whole),
        [ANY] * 2,
        [SMEM] + [VMEM] * 11,
        [
            half,
            half,
            half,
            half,
            pltpu.VMEM((S, 3 * S), BF),
            pltpu.VMEM((S, S), BF),
            pltpu.VMEM((S, S), BF),
            pltpu.VMEM((S, S), F32),
            pltpu.VMEM(ymatrix.shape, BF),
            pltpu.VMEM(ymatrix.shape, BF),
            pltpu.SemaphoreType.DMA((8,)),
        ],
        20 * S**3,
        (pattern, yw, zw, td, r1, l1, r2, l2, r3, l3, e, l),
    )


def solution(mesh):
    band = P(AXES, None, None, None)
    return jax.shard_map(
        local,
        mesh=mesh,
        in_specs=(band, band, P(AXES, None)),
        out_specs=(band, band),
        check_vma=False,
    )
```

```python
import jax
import jax.numpy as jnp
from jax import lax
from jax.experimental import pallas as pl
from jax.experimental.pallas import tpu as pltpu
from jax.sharding import PartitionSpec as P

AXES = ("row", "col")
B = 128
S = 512
H = 256
RING = 8
BF = jnp.bfloat16
F32 = jnp.float32

LOWER = [(r, c) for r in range(4) for c in range(r, 4)]
UPPER = [(r, c) for r in range(4) for c in range(r)]
FULL = [(r, c) for r in range(4) for c in range(4)]


def of(name, blocks):
    return [(name, r, c) for r, c in blocks]


R1 = of("yU", UPPER)
L1 = of("yL", LOWER)
L_TOP = [p for p in LOWER if p[0] < 3]
R_REST = of("yD", FULL) + of("zU", UPPER) + of("zD", FULL)
L_REST = of("yD", [(r, c) for r in range(3) for c in range(3)]) + of("zL", L_TOP) + of("zD", FULL[:12])
R2, R3 = R_REST[:16], R_REST[16:]
L2, L3 = of("sum", UPPER) + L_REST[:13], L_REST[13:]
COLUMN = {"L": 0, "D": S, "U": 2 * S}
QUADS = {
    "L": ((0, 0), (0, 1), (1, 1)),
    "D": ((0, 0), (0, 1), (1, 0), (1, 1)),
    "U": ((0, 0), (1, 0), (1, 1)),
}
BLOCKS = {"L": LOWER, "D": FULL, "U": UPPER}


def slot(part, r, c):
    return c - r + {"L": 0, "D": 4, "U": 8}[part]


def rows(i, n=1):
    return pl.ds(i * B, n * B)


def unpack(message, ref, into):
    for i, (name, r, c) in enumerate(message):
        if into[name] is None:
            continue
        target, column = into[name]
        target[rows(r), pl.ds(column + c * B, B)] = ref[rows(i), :]


def clear(target, column, blocks):
    for r, c in FULL:
        if (r, c) not in blocks:
            target[rows(r), pl.ds(column + c * B, B)] = jnp.zeros((B, B), target.dtype)


def product(acc, part, *terms, base=None):
    for i, n in QUADS[part]:
        total = None if base is None else base[pl.ds(i * H, H), pl.ds(n * H, H)]
        for (left, lc, lp), (right, rc, rp) in terms:
            ks = [k for k in (0, 1) if (i, k) in QUADS[lp] and (k, n) in QUADS[rp]]
            if not ks:
                continue
            low, size = ks[0] * H, len(ks) * H
            value = jnp.dot(
                left[pl.ds(i * H, H), pl.ds(lc + low, size)],
                right[pl.ds(low, size), pl.ds(rc + n * H, H)],
                preferred_element_type=F32,
            )
            total = value if total is None else total + value
        acc[pl.ds(i * H, H), pl.ds(n * H, H)] = total


def side(ref, part, column=None):
    return ref, COLUMN[part] if column is None else column, part


def keep(pattern, part, r, c):
    d = slot(part, r, c)
    return True if d == 4 else pattern[r, d] == 1


def masked(flag, block):
    return block if flag is True else jnp.where(flag, block, jnp.zeros_like(block))


def pack_kernel(edge, pattern, y, z, r1, l1, r2, r3, l3, zz, yw, zw, yin, zin, sems):
    copies = []
    for i, (source, target) in enumerate(((y, yin), (z, zin))):
        for r in range(4):
            copies.append(pltpu.make_async_copy(source.at[r], target.at[r], sems.at[i * 4 + r]))
            copies[-1].start()
    for copy in copies:
        copy.wait()
    for wide, source in ((yw, yin), (zw, zin)):
        for r in range(4):
            for d in range(8):
                k = True if d == 4 else pattern[r, d] == 1
                wide[rows(r), rows(r + d)] = masked(k, source[r, d])
            for c in range(12):
                if not r <= c < r + 8:
                    wide[rows(r), rows(c)] = jnp.zeros((B, B), BF)

    def fill(message, ref):
        for i, (name, r, c) in enumerate(message):
            wide = yw if name[0] == "y" else zw
            ref[rows(i), :] = wide[rows(r), pl.ds(COLUMN[name[1]] + c * B, B)]

    for message, ref in ((R1, r1), (L1, l1), (R2, r2), (R3, r3), (L3, l3)):
        fill(message, ref)

    @pl.when(edge[0] == 1)
    def _():
        fill(L3, zz)

    @pl.when(edge[0] == 0)
    def _():
        fill(R3, zz)

    line = lax.broadcasted_iota(jnp.int32, (16, B), 0)
    for message, ref in ((R1, r1), (L1, l1)):
        tile = jnp.zeros((16, B), F32)
        for i, (name, r, c) in enumerate(message):
            k = keep(pattern, name[1], r, c)
            tile = jnp.where(line == i, 1.0 if k is True else jnp.where(k, 1.0, 0.0), tile)
        ref[pl.ds(len(message) * B, 16), :] = tile.astype(BF)


def middle_kernel(pattern, yw, zw, r1, l1, td, e, l, yu, yl, acc):
    clear(yu, 0, UPPER)
    clear(yl, 0, LOWER)
    unpack(R1, r1, {"yU": (yu, 0)})
    unpack(L1, l1, {"yL": (yl, 0)})
    product(
        acc,
        "D",
        (side(zw, "L"), side(yu, "U", 0)),
        (side(zw, "D"), side(yw, "D")),
        (side(zw, "U"), side(yl, "L", 0)),
    )
    eye = jnp.where(
        lax.broadcasted_iota(jnp.int32, (B, B), 0) == lax.broadcasted_iota(jnp.int32, (B, B), 1), 1.5, 0.0
    )
    for r, c in FULL:
        block = -0.5 * acc[rows(r), rows(c)]
        if r == c:
            block = block + eye
        td[rows(r), rows(c)] = masked(keep(pattern, "D", r, c), block).astype(BF)
    for part, left, out in (("L", yl, e), ("U", yu, l)):
        product(acc, part, (side(left, part, 0), side(td, "D", 0)))
        for i, (r, c) in enumerate(BLOCKS[part]):
            out[rows(i), :] = acc[rows(r), rows(c)].astype(BF)
    for i, (name, r, c) in enumerate(L2):
        if name != "sum":
            wide = yw if name[0] == "y" else zw
            l[rows(i), :] = wide[rows(r), pl.ds(COLUMN[name[1]] + c * B, B)]


def relay_kernel(edge, zz, after, r3, l3, r3_out, l3_out):
    @pl.when(edge[1] == 1)
    def _():
        r3_out[...] = zz[...]

    @pl.when(edge[0] == 1)
    def _():
        l3_out[...] = zz[pl.ds(0, len(L3) * B), :]


def own_kernel(pattern, yw, zw, td, r2, tl, *rest):
    *sums, ya, acc = rest
    unpack(R2, r2, {"yD": (ya, 0), "zU": None})
    clear(tl, 0, LOWER)
    y_d, z_d, t_d = side(yw, "D"), side(zw, "D"), side(td, "D", 0)
    product(acc, "L", (side(zw, "L"), side(ya, "D", 0)), (z_d, side(yw, "L")))
    for r, c in LOWER:
        tl[rows(r), rows(c)] = masked(keep(pattern, "L", r, c), -0.5 * acc[rows(r), rows(c)]).astype(BF)
    zl, zd, zu, yl, yd, zy = sums
    product(zl, "L", (t_d, side(zw, "L")))
    product(zd, "D", (t_d, z_d))
    product(zu, "U", (t_d, side(zw, "U")))
    product(yl, "L", (y_d, side(tl, "L", 0)))
    product(yd, "D", (y_d, t_d))
    product(zy, "U", (z_d, side(yw, "U")))


def late_kernel(pattern, yw, zw, zy, yl, e, l2, tu, yu, yl_out, yc, acc):
    unpack(L2, l2, {"yD": (yc, 0), "zL": None, "sum": None})
    clear(yc, 0, [(r, c) for r in range(3) for c in range(3)])
    clear(tu, 0, UPPER)
    product(acc, "U", (side(zw, "U"), side(yc, "D", 0)), base=zy)
    for r, c in UPPER:
        tu[rows(r), rows(c)] = masked(keep(pattern, "U", r, c), -0.5 * acc[rows(r), rows(c)]).astype(BF)
    product(yu, "U", (side(yw, "D"), side(tu, "U", 0)))
    for total, blocks, message in ((yl_out, LOWER, e), (yu, UPPER, l2)):
        for i, (r, c) in enumerate(blocks):
            total[rows(r), rows(c)] += message[rows(i), :].astype(F32)


def last_kernel(pattern, yw, tl, tu, zl, zd, zu, yl, yd, yu, r1, l1, r2, l2, r3, l3, yout, zout, *scratch):
    yu_a, yl_c, za, zc, tua, tlc, acc, yo, zo, sems = scratch
    clear(yu_a, 0, UPPER)
    clear(za, S, UPPER)
    clear(yl_c, 0, LOWER)
    clear(zc, 0, L_TOP)
    clear(zc, S, FULL[:12])
    left = {"yD": None, "yU": (yu_a, 0), "zD": (za, 0), "zU": (za, S)}
    right = {"yL": (yl_c, 0), "yD": None, "zL": (zc, 0), "zD": (zc, S), "sum": None}
    for message, ref in ((R1, r1), (R2, r2), (R3, r3)):
        unpack(message, ref, left)
    for message, ref in ((L1, l1), (L2, l2), (L3, l3)):
        unpack(message, ref, right)
    clear(tua, 0, UPPER)
    clear(tlc, 0, L_TOP)
    copies = []

    def write(source, target):
        for r in range(4):
            copies.append(pltpu.make_async_copy(source.at[r], target.at[r], sems.at[len(copies)]))
            copies[-1].start()

    def finish(out, part, *terms, base):
        if terms:
            product(acc, part, *terms, base=base)
        for r, c in BLOCKS[part]:
            block = (acc if terms else base)[rows(r), rows(c)]
            out[r, slot(part, r, c)] = masked(keep(pattern, part, r, c), block).astype(BF)

    t_l, t_u = side(tl, "L", 0), side(tu, "U", 0)
    finish(zo, "L", (t_l, side(za, "D", 0)), base=zl)
    finish(zo, "D", (t_l, side(za, "U", S)), (t_u, side(zc, "L", 0)), base=zd)
    finish(zo, "U", (t_u, side(zc, "D", S)), base=zu)
    write(zo, zout)
    left_mask = r1[pl.ds(len(R1) * B, 16), :].astype(F32)
    right_mask = l1[pl.ds(len(L1) * B, 16), :].astype(F32)
    product(acc, "U", (side(za, "D", 0), side(yu_a, "U", 0)), (side(za, "U", S), side(yw, "D")))
    for i, (r, c) in enumerate(UPPER):
        tua[rows(r), rows(c)] = (-0.5 * acc[rows(r), rows(c)] * left_mask[i : i + 1, :]).astype(BF)
    product(acc, "L", (side(zc, "L", 0), side(yw, "D")), (side(zc, "D", S), side(yl_c, "L", 0)))
    for i, (r, c) in enumerate(LOWER):
        if r < 3:
            tlc[rows(r), rows(c)] = (-0.5 * acc[rows(r), rows(c)] * right_mask[i : i + 1, :]).astype(BF)
    finish(yo, "D", (side(yw, "L"), side(tua, "U", 0)), (side(yw, "U"), side(tlc, "L", 0)), base=yd)
    finish(yo, "L", base=yl)
    finish(yo, "U", base=yu)
    write(yo, yout)
    for copy in copies:
        copy.wait()


VMEM = pl.BlockSpec(memory_space=pltpu.VMEM)
SMEM = pl.BlockSpec(memory_space=pltpu.SMEM)
ANY = pl.BlockSpec(memory_space=pl.ANY)
HBM = pl.BlockSpec(memory_space=pltpu.HBM)


def packed(blocks, masks=False):
    return jax.ShapeDtypeStruct((len(blocks) * B + 16 * masks, B), BF)


def call(kernel, outs, out_specs, ins, scratch, flops, operands, **options):
    outs = tuple(outs)
    moved = sum(v.size * v.dtype.itemsize for v in (*outs, *operands))
    return pl.pallas_call(
        kernel,
        out_shape=outs,
        in_specs=ins,
        out_specs=tuple(out_specs),
        scratch_shapes=scratch,
        compiler_params=pltpu.CompilerParams(vmem_limit_bytes=VMEM_LIMIT),
        cost_estimate=pl.CostEstimate(flops=flops, bytes_accessed=moved, transcendentals=0),
        **options,
    )(*operands)


VMEM_LIMIT = 24 * 2**20


def local(ymatrix, zmatrix, pattern):
    count = lax.axis_size("row") * lax.axis_size("col")
    place = lax.axis_index("col") % RING
    first, last = place == 0, place == RING - 1
    right = [(i, (i + 1) % count) for i in range(count)]
    left = [(b, a) for a, b in right]
    ends = [(i, (i + RING) % count) for i in range(count) if i % RING == RING - 1]
    ends += [((i + RING) % count, i) for i in range(count) if i % RING == 0]
    right_y = [(i, i + 1 if i % RING < RING - 1 else i - RING + 1) for i in range(count)]
    left_y = [(b, a) for a, b in right_y]

    def send(x, pairs):
        return lax.ppermute(x, AXES, pairs)

    wide = jax.ShapeDtypeStruct((S, 3 * S), BF)
    edge = jnp.stack([first, last]).astype(jnp.int32)
    r1, l1, r2, r3, l3, zz, yw, zw = call(
        pack_kernel,
        (packed(R1, True), packed(L1, True)) + tuple(packed(m) for m in (R2, R3, L3, R3)) + (wide, wide),
        [VMEM] * 8,
        [SMEM, SMEM, HBM, HBM],
        [
            pltpu.VMEM(ymatrix.shape, BF),
            pltpu.VMEM(ymatrix.shape, BF),
            pltpu.SemaphoreType.DMA((8,)),
        ],
        0,
        (edge, pattern, ymatrix, zmatrix),
    )
    r1, l1 = send(r1, right), send(l1, left)
    zz = send(zz, ends)
    r2 = send(r2, right)
    td, e, l2 = call(
        middle_kernel,
        (jax.ShapeDtypeStruct((S, S), BF), packed(LOWER), packed(L2)),
        [VMEM] * 3,
        [SMEM] + [VMEM] * 4,
        [pltpu.VMEM((S, S), BF), pltpu.VMEM((S, S), BF), pltpu.VMEM((S, S), F32)],
        6 * S**3,
        (pattern, yw, zw, r1, l1),
    )
    e, l2 = send(e, right), send(l2, left)
    r3, l3 = call(
        relay_kernel,
        (packed(R3), packed(L3)),
        [VMEM] * 2,
        [SMEM, VMEM, ANY, VMEM, VMEM],
        [],
        0,
        (edge, zz, td, r3, l3),
        input_output_aliases={3: 0, 4: 1},
    )
    r3, l3 = send(r3, right_y), send(l3, left_y)
    square, total = jax.ShapeDtypeStruct((S, S), BF), jax.ShapeDtypeStruct((S, S), F32)
    one, half = pltpu.VMEM((S, S), BF), pltpu.VMEM((S, 2 * S), BF)
    full = pltpu.VMEM((S, S), F32)
    tl, zl, zd, zu, yl, yd, zy = call(
        own_kernel,
        (square,) + (total,) * 6,
        [VMEM] * 7,
        [SMEM] + [VMEM] * 4,
        [one, full],
        10 * S**3,
        (pattern, yw, zw, td, r2),
    )
    tu, yu, yl = call(
        late_kernel,
        (square, total, total),
        [VMEM] * 3,
        [SMEM] + [VMEM] * 6,
        [one, full],
        50 * S**3,
        (pattern, yw, zw, zy, yl, e, l2),
        input_output_aliases={4: 2},
    )
    whole = jax.ShapeDtypeStruct(ymatrix.shape, BF)
    block_rows = pltpu.VMEM(ymatrix.shape, BF)
    return call(
        last_kernel,
        (whole, whole),
        [ANY] * 2,
        [SMEM] + [VMEM] * 15,
        [one, one, half, half, one, one, full, block_rows, block_rows, pltpu.SemaphoreType.DMA((8,))],
        10 * S**3,
        (pattern, yw, tl, tu, zl, zd, zu, yl, yd, yu, r1, l1, r2, l2, r3, l3),
    )


def solution(mesh):
    band = P(AXES, None, None, None)
    return jax.shard_map(
        local,
        mesh=mesh,
        in_specs=(band, band, P(AXES, None)),
        out_specs=(band, band),
        check_vma=False,
    )
```

```python
import jax
import jax.numpy as jnp
from jax import lax
from jax.experimental import pallas as pl
from jax.experimental.pallas import tpu as pltpu
from jax.sharding import PartitionSpec as P

AXES = ("row", "col")
B = 128
S = 512
H = 256
RING = 8
BF = jnp.bfloat16
F32 = jnp.float32

LOWER = [(r, c) for r in range(4) for c in range(r, 4)]
UPPER = [(r, c) for r in range(4) for c in range(r)]
FULL = [(r, c) for r in range(4) for c in range(4)]


def of(name, blocks):
    return [(name, r, c) for r, c in blocks]


R1 = of("yU", UPPER)
L1 = of("yL", LOWER)
L_TOP = [p for p in LOWER if p[0] < 3]
R_REST = of("yD", FULL) + of("zU", UPPER) + of("zD", FULL)
L_REST = of("yD", [(r, c) for r in range(3) for c in range(3)]) + of("zL", L_TOP) + of("zD", FULL[:12])
R2, R3 = R_REST[:18], R_REST[18:]
L2, L3 = of("sum", UPPER) + L_REST[:15], L_REST[15:]
COLUMN = {"L": 0, "D": S, "U": 2 * S}
QUADS = {
    "L": ((0, 0), (0, 1), (1, 1)),
    "D": ((0, 0), (0, 1), (1, 0), (1, 1)),
    "U": ((0, 0), (1, 0), (1, 1)),
}
BLOCKS = {"L": LOWER, "D": FULL, "U": UPPER}


def slot(part, r, c):
    return c - r + {"L": 0, "D": 4, "U": 8}[part]


def rows(i, n=1):
    return pl.ds(i * B, n * B)


def unpack(message, ref, into):
    for i, (name, r, c) in enumerate(message):
        if into[name] is None:
            continue
        target, column = into[name]
        target[rows(r), pl.ds(column + c * B, B)] = ref[rows(i), :]


def clear(target, column, blocks):
    for r, c in FULL:
        if (r, c) not in blocks:
            target[rows(r), pl.ds(column + c * B, B)] = jnp.zeros((B, B), target.dtype)


def product(acc, part, *terms, base=None):
    for i, n in QUADS[part]:
        total = None if base is None else base[pl.ds(i * H, H), pl.ds(n * H, H)]
        for (left, lc, lp), (right, rc, rp) in terms:
            ks = [k for k in (0, 1) if (i, k) in QUADS[lp] and (k, n) in QUADS[rp]]
            if not ks:
                continue
            low, size = ks[0] * H, len(ks) * H
            value = jnp.dot(
                left[pl.ds(i * H, H), pl.ds(lc + low, size)],
                right[pl.ds(low, size), pl.ds(rc + n * H, H)],
                preferred_element_type=F32,
            )
            total = value if total is None else total + value
        acc[pl.ds(i * H, H), pl.ds(n * H, H)] = total


def side(ref, part, column=None):
    return ref, COLUMN[part] if column is None else column, part


def keep(pattern, part, r, c):
    d = slot(part, r, c)
    return True if d == 4 else pattern[r, d] == 1


def masked(flag, block):
    return block if flag is True else jnp.where(flag, block, jnp.zeros_like(block))


def pack_kernel(pattern_in, y, z, r1, l1, r2, r3, l3, zz, yw, zw, yin, zin, pattern, sems):
    place = lax.rem(lax.axis_index("col"), RING)
    copies = [pltpu.make_async_copy(pattern_in, pattern, sems.at[8])]
    for i, (source, target) in enumerate(((y, yin), (z, zin))):
        for r in range(4):
            copies.append(pltpu.make_async_copy(source.at[r], target.at[r], sems.at[i * 4 + r]))
    for copy in copies:
        copy.start()
    copies[0].wait()
    for i, (wide, source) in enumerate(((yw, yin), (zw, zin))):
        for r in range(4):
            for c in range(12):
                if not r <= c < r + 8:
                    wide[rows(r), rows(c)] = jnp.zeros((B, B), BF)
            copies[1 + i * 4 + r].wait()
            for d in range(8):
                k = True if d == 4 else pattern[r, d] == 1
                wide[rows(r), rows(r + d)] = masked(k, source[r, d])

    def fill(message, ref):
        for i, (name, r, c) in enumerate(message):
            wide = yw if name[0] == "y" else zw
            ref[rows(i), :] = wide[rows(r), pl.ds(COLUMN[name[1]] + c * B, B)]

    for message, ref in ((R1, r1), (L1, l1), (R2, r2), (R3, r3), (L3, l3)):
        fill(message, ref)

    @pl.when(place == 0)
    def _():
        fill(L3, zz)

    @pl.when(place == RING - 1)
    def _():
        fill(R3, zz)

    line = lax.broadcasted_iota(jnp.int32, (16, B), 0)
    for message, ref in ((R1, r1), (L1, l1)):
        tile = jnp.zeros((16, B), F32)
        for i, (name, r, c) in enumerate(message):
            k = keep(pattern, name[1], r, c)
            tile = jnp.where(line == i, 1.0 if k is True else jnp.where(k, 1.0, 0.0), tile)
        ref[pl.ds(len(message) * B, 16), :] = tile.astype(BF)


def middle_kernel(pattern, yw, zw, r1, l1, td, e, l, yu, yl, acc):
    clear(yu, 0, UPPER)
    clear(yl, 0, LOWER)
    unpack(R1, r1, {"yU": (yu, 0)})
    unpack(L1, l1, {"yL": (yl, 0)})
    product(
        acc,
        "D",
        (side(zw, "L"), side(yu, "U", 0)),
        (side(zw, "D"), side(yw, "D")),
        (side(zw, "U"), side(yl, "L", 0)),
    )
    eye = jnp.where(
        lax.broadcasted_iota(jnp.int32, (B, B), 0) == lax.broadcasted_iota(jnp.int32, (B, B), 1), 1.5, 0.0
    )
    for r, c in FULL:
        block = -0.5 * acc[rows(r), rows(c)]
        if r == c:
            block = block + eye
        td[rows(r), rows(c)] = masked(keep(pattern, "D", r, c), block).astype(BF)
    for part, left, out in (("L", yl, e), ("U", yu, l)):
        product(acc, part, (side(left, part, 0), side(td, "D", 0)))
        for i, (r, c) in enumerate(BLOCKS[part]):
            out[rows(i), :] = acc[rows(r), rows(c)].astype(BF)
    for i, (name, r, c) in enumerate(L2):
        if name != "sum":
            wide = yw if name[0] == "y" else zw
            l[rows(i), :] = wide[rows(r), pl.ds(COLUMN[name[1]] + c * B, B)]


def relay_kernel(zz, after, r3, l3, r3_out, l3_out):
    place = lax.rem(lax.axis_index("col"), RING)

    @pl.when(place == RING - 1)
    def _():
        r3_out[...] = zz[pl.ds(0, len(R3) * B), :]

    @pl.when(place != RING - 1)
    def _():
        r3_out[...] = r3[...]

    @pl.when(place == 0)
    def _():
        l3_out[...] = zz[pl.ds(0, len(L3) * B), :]

    @pl.when(place != 0)
    def _():
        l3_out[...] = l3[...]


def own_kernel(pattern, yw, zw, td, r2, tl, *rest):
    *sums, ya, acc = rest
    unpack(R2, r2, {"yD": (ya, 0), "zU": None})
    clear(tl, 0, LOWER)
    y_d, z_d, t_d = side(yw, "D"), side(zw, "D"), side(td, "D", 0)
    product(acc, "L", (side(zw, "L"), side(ya, "D", 0)), (z_d, side(yw, "L")))
    for r, c in LOWER:
        tl[rows(r), rows(c)] = masked(keep(pattern, "L", r, c), -0.5 * acc[rows(r), rows(c)]).astype(BF)
    zl, zd, zu, yl, yd, zy = sums
    product(zl, "L", (t_d, side(zw, "L")))
    product(zd, "D", (t_d, z_d))
    product(zu, "U", (t_d, side(zw, "U")))
    product(yl, "L", (y_d, side(tl, "L", 0)))
    product(yd, "D", (y_d, t_d))
    product(zy, "U", (z_d, side(yw, "U")))


def finish(pattern, out, total, part, extra=None):
    for i, (r, c) in enumerate(BLOCKS[part]):
        block = total[rows(r), rows(c)]
        if extra is not None:
            block = block + extra[rows(i), :].astype(F32)
        out[i] = masked(keep(pattern, part, r, c), block).astype(BF)


def late_kernel(pattern, yw, zw, zy, yl, e, l2, tu, yl_out, yu_out, yc, acc):
    unpack(L2, l2, {"yD": (yc, 0), "zL": None, "sum": None})
    clear(yc, 0, [(r, c) for r in range(3) for c in range(3)])
    clear(tu, 0, UPPER)
    finish(pattern, yl_out, yl, "L", e)
    product(acc, "U", (side(zw, "U"), side(yc, "D", 0)), base=zy)
    for r, c in UPPER:
        tu[rows(r), rows(c)] = masked(keep(pattern, "U", r, c), -0.5 * acc[rows(r), rows(c)]).astype(BF)
    product(acc, "U", (side(yw, "D"), side(tu, "U", 0)))
    finish(pattern, yu_out, acc, "U", l2)


def right_kernel(pattern, yw, tu, zd, zu, yd, l1, l2, l3, zu_out, zd_out, yd_out, yl, zl_c, zd_c, tlc, acc):
    clear(yl, 0, LOWER)
    clear(zl_c, 0, L_TOP)
    clear(zd_c, 0, FULL[:12])
    for message, ref in ((L1, l1), (L2, l2), (L3, l3)):
        unpack(message, ref, {"yL": (yl, 0), "yD": None, "zL": (zl_c, 0), "zD": (zd_c, 0), "sum": None})
    clear(tlc, 0, L_TOP)
    mask = l1[pl.ds(len(L1) * B, 16), :].astype(F32)
    product(acc, "L", (side(zl_c, "L", 0), side(yw, "D")), (side(zd_c, "D", 0), side(yl, "L", 0)))
    for i, (r, c) in enumerate(LOWER):
        if r < 3:
            tlc[rows(r), rows(c)] = (-0.5 * acc[rows(r), rows(c)] * mask[i : i + 1, :]).astype(BF)
    t_u = side(tu, "U", 0)
    product(acc, "U", (t_u, side(zd_c, "D", 0)), base=zu)
    finish(pattern, zu_out, acc, "U")
    product(zd_out, "D", (t_u, side(zl_c, "L", 0)), base=zd)
    product(yd_out, "D", (side(yw, "U"), side(tlc, "L", 0)), base=yd)


def last_kernel(pattern, yw, tl, zl, zd, zu, yl, yd, yu, r1, r2, r3, yout, zout, *scratch):
    yu_a, zu_a, zd_a, tua, acc, y_d, z_d, z_l, sems = scratch
    copies = []

    def write(source, target, part):
        at = 0
        for r in range(4):
            size, d = {"L": (4 - r, 0), "D": (4, 4 - r), "U": (r, 8 - r)}[part]
            if size:
                copies.append(
                    pltpu.make_async_copy(
                        source.at[pl.ds(at, size)], target.at[r, pl.ds(d, size)], sems.at[len(copies)]
                    )
                )
                copies[-1].start()
            at += size

    write(zu, zout, "U")
    write(yl, yout, "L")
    write(yu, yout, "U")
    clear(yu_a, 0, UPPER)
    clear(zu_a, 0, UPPER)
    for message, ref in ((R1, r1), (R2, r2), (R3, r3)):
        unpack(message, ref, {"yD": None, "yU": (yu_a, 0), "zD": (zd_a, 0), "zU": (zu_a, 0)})
    clear(tua, 0, UPPER)
    mask = r1[pl.ds(len(R1) * B, 16), :].astype(F32)
    t_l = side(tl, "L", 0)
    product(acc, "D", (t_l, side(zu_a, "U", 0)), base=zd)
    finish(pattern, z_d, acc, "D")
    write(z_d, zout, "D")
    product(acc, "U", (side(zd_a, "D", 0), side(yu_a, "U", 0)), (side(zu_a, "U", 0), side(yw, "D")))
    for i, (r, c) in enumerate(UPPER):
        tua[rows(r), rows(c)] = (-0.5 * acc[rows(r), rows(c)] * mask[i : i + 1, :]).astype(BF)
    product(acc, "D", (side(yw, "L"), side(tua, "U", 0)), base=yd)
    finish(pattern, y_d, acc, "D")
    write(y_d, yout, "D")
    product(acc, "L", (t_l, side(zd_a, "D", 0)), base=zl)
    finish(pattern, z_l, acc, "L")
    write(z_l, zout, "L")
    for copy in copies:
        copy.wait()


VMEM = pl.BlockSpec(memory_space=pltpu.VMEM)
SMEM = pl.BlockSpec(memory_space=pltpu.SMEM)
ANY = pl.BlockSpec(memory_space=pl.ANY)
HBM = pl.BlockSpec(memory_space=pltpu.HBM)


def packed(blocks, masks=False):
    return jax.ShapeDtypeStruct((len(blocks) * B + 16 * masks, B), BF)


def call(kernel, outs, out_specs, ins, scratch, flops, operands, **options):
    outs = tuple(outs)
    moved = sum(v.size * v.dtype.itemsize for v in (*outs, *operands))
    return pl.pallas_call(
        kernel,
        out_shape=outs,
        in_specs=ins,
        out_specs=tuple(out_specs),
        scratch_shapes=scratch,
        compiler_params=pltpu.CompilerParams(vmem_limit_bytes=VMEM_LIMIT),
        cost_estimate=pl.CostEstimate(flops=flops, bytes_accessed=moved, transcendentals=0),
        **options,
    )(*operands)


VMEM_LIMIT = 24 * 2**20
OWN_COST, LATE_COST, RIGHT_COST = 10, 35, 5


def local(ymatrix, zmatrix, pattern):
    count = lax.axis_size("row") * lax.axis_size("col")
    right = [(i, (i + 1) % count) for i in range(count)]
    left = [(b, a) for a, b in right]
    ends = [(i, (i + RING) % count) for i in range(count) if i % RING == RING - 1]
    ends += [((i + RING) % count, i) for i in range(count) if i % RING == 0]
    right_y = [(i, i + 1 if i % RING < RING - 1 else i - RING + 1) for i in range(count)]
    left_y = [(b, a) for a, b in right_y]

    def send(x, pairs):
        return lax.ppermute(x, AXES, pairs)

    wide = jax.ShapeDtypeStruct((S, 3 * S), BF)
    r1, l1, r2, r3, l3, zz, yw, zw = call(
        pack_kernel,
        (packed(R1, True), packed(L1, True)) + tuple(packed(m) for m in (R2, R3, L3, max(R3, L3, key=len))) + (wide, wide),
        [VMEM] * 8,
        [HBM] * 3,
        [
            pltpu.VMEM(ymatrix.shape, BF),
            pltpu.VMEM(ymatrix.shape, BF),
            pltpu.SMEM(pattern.shape, jnp.int32),
            pltpu.SemaphoreType.DMA((9,)),
        ],
        0,
        tuple(pltpu.with_memory_space_constraint(v, pltpu.HBM) for v in (pattern, ymatrix, zmatrix)),
    )
    r1, l1 = send(r1, right), send(l1, left)
    zz = send(zz, ends)
    r2 = send(r2, right)
    td, e, l2 = call(
        middle_kernel,
        (jax.ShapeDtypeStruct((S, S), BF), packed(LOWER), packed(L2)),
        [VMEM] * 3,
        [SMEM] + [VMEM] * 4,
        [pltpu.VMEM((S, S), BF), pltpu.VMEM((S, S), BF), pltpu.VMEM((S, S), F32)],
        6 * S**3,
        (pattern, yw, zw, r1, l1),
    )
    e, l2 = send(e, right), send(l2, left)
    r3, l3 = call(
        relay_kernel,
        (packed(R3), packed(L3)),
        [VMEM] * 2,
        [VMEM, ANY, VMEM, VMEM],
        [],
        0,
        (zz, td, r3, l3),
    )
    r3, l3 = send(r3, right_y), send(l3, left_y)
    square, total = jax.ShapeDtypeStruct((S, S), BF), jax.ShapeDtypeStruct((S, S), F32)
    one, half = pltpu.VMEM((S, S), BF), pltpu.VMEM((S, 2 * S), BF)
    full = pltpu.VMEM((S, S), F32)
    tl, zl, zd, zu, yl, yd, zy = call(
        own_kernel,
        (square,) + (total,) * 6,
        [VMEM] * 7,
        [SMEM] + [VMEM] * 4,
        [one, full],
        OWN_COST * S**3,
        (pattern, yw, zw, td, r2),
    )
    lower, upper = (jax.ShapeDtypeStruct((len(v), B, B), BF) for v in (LOWER, UPPER))
    tu, yl, yu = call(
        late_kernel,
        (square, lower, upper),
        [VMEM] * 3,
        [SMEM] + [VMEM] * 6,
        [one, full],
        LATE_COST * S**3,
        (pattern, yw, zw, zy, yl, e, l2),
    )
    zu, zd, yd = call(
        right_kernel,
        (upper, total, total),
        [VMEM] * 3,
        [SMEM] + [VMEM] * 8,
        [one, one, one, one, full],
        RIGHT_COST * S**3,
        (pattern, yw, tu, zd, zu, yd, l1, l2, l3),
        input_output_aliases={3: 1, 5: 2},
    )
    whole = jax.ShapeDtypeStruct(ymatrix.shape, BF)
    return call(
        last_kernel,
        (whole, whole),
        [ANY] * 2,
        [SMEM] + [VMEM] * 11,
        [
            one,
            one,
            one,
            one,
            full,
            pltpu.VMEM((16, B, B), BF),
            pltpu.VMEM((16, B, B), BF),
            pltpu.VMEM((10, B, B), BF),
            pltpu.SemaphoreType.DMA((22,)),
        ],
        10 * S**3,
        (pattern, yw, tl, zl, zd, zu, yl, yd, yu, r1, r2, r3),
    )


def solution(mesh):
    band = P(AXES, None, None, None)
    return jax.shard_map(
        local,
        mesh=mesh,
        in_specs=(band, band, P(AXES, None)),
        out_specs=(band, band),
        check_vma=False,
    )
```

```python
import jax
import jax.numpy as jnp
from jax import lax
from jax.experimental import pallas as pl
from jax.experimental.pallas import tpu as pltpu
from jax.sharding import PartitionSpec as P

AXES = ("row", "col")
B = 128
S = 512
H = 256
RING = 8
BF = jnp.bfloat16
F32 = jnp.float32

LOWER = [(r, c) for r in range(4) for c in range(r, 4)]
UPPER = [(r, c) for r in range(4) for c in range(r)]
FULL = [(r, c) for r in range(4) for c in range(4)]


def of(name, blocks):
    return [(name, r, c) for r, c in blocks]


R1 = of("yU", UPPER)
L1 = of("yL", LOWER)
L_TOP = [p for p in LOWER if p[0] < 3]
R_REST = of("yD", FULL) + of("zU", UPPER) + of("zD", FULL)
L_REST = of("yD", [(r, c) for r in range(3) for c in range(3)]) + of("zL", L_TOP) + of("zD", FULL[:12])
R2, R3 = R_REST[:19], R_REST[19:]
L2, L3 = of("sum", UPPER) + L_REST[:15], L_REST[15:]
COLUMN = {"L": 0, "D": S, "U": 2 * S}
QUADS = {
    "L": ((0, 0), (0, 1), (1, 1)),
    "D": ((0, 0), (0, 1), (1, 0), (1, 1)),
    "U": ((0, 0), (1, 0), (1, 1)),
}
BLOCKS = {"L": LOWER, "D": FULL, "U": UPPER}


def slot(part, r, c):
    return c - r + {"L": 0, "D": 4, "U": 8}[part]


def rows(i, n=1):
    return pl.ds(i * B, n * B)


def unpack(message, ref, into):
    for i, (name, r, c) in enumerate(message):
        if into[name] is None:
            continue
        target, column = into[name]
        target[rows(r), pl.ds(column + c * B, B)] = ref[rows(i), :]


def clear(target, column, blocks):
    for r, c in FULL:
        if (r, c) not in blocks:
            target[rows(r), pl.ds(column + c * B, B)] = jnp.zeros((B, B), target.dtype)


def product(acc, part, *terms, base=None):
    for i, n in QUADS[part]:
        total = None if base is None else base[pl.ds(i * H, H), pl.ds(n * H, H)]
        for (left, lc, lp), (right, rc, rp) in terms:
            ks = [k for k in (0, 1) if (i, k) in QUADS[lp] and (k, n) in QUADS[rp]]
            if not ks:
                continue
            low, size = ks[0] * H, len(ks) * H
            value = jnp.dot(
                left[pl.ds(i * H, H), pl.ds(lc + low, size)],
                right[pl.ds(low, size), pl.ds(rc + n * H, H)],
                preferred_element_type=F32,
            )
            total = value if total is None else total + value
        acc[pl.ds(i * H, H), pl.ds(n * H, H)] = total


def side(ref, part, column=None):
    return ref, COLUMN[part] if column is None else column, part


def keep(pattern, part, r, c):
    d = slot(part, r, c)
    return True if d == 4 else pattern[r, d] == 1


def masked(flag, block):
    return block if flag is True else jnp.where(flag, block, jnp.zeros_like(block))


def widen(pattern, wide, source, ready):
    for r in range(4):
        for c in range(12):
            if not r <= c < r + 8:
                wide[rows(r), rows(c)] = jnp.zeros((B, B), BF)
        ready(r)
        for d in range(8):
            k = True if d == 4 else pattern[r, d] == 1
            wide[rows(r), rows(r + d)] = masked(k, source[r, d])


def fill(message, ref, yw, zw):
    for i, (name, r, c) in enumerate(message):
        wide = yw if name[0] == "y" else zw
        ref[rows(i), :] = wide[rows(r), pl.ds(COLUMN[name[1]] + c * B, B)]


def first_kernel(pattern_in, y, z, r1, l1, yw, zin, yin, pattern, sems):
    copies = [pltpu.make_async_copy(pattern_in, pattern, sems.at[8])]
    for i, (source, target) in enumerate(((y, yin), (z, zin))):
        for r in range(4):
            copies.append(pltpu.make_async_copy(source.at[r], target.at[r], sems.at[i * 4 + r]))
    for copy in copies:
        copy.start()
    copies[0].wait()
    widen(pattern, yw, yin, lambda r: copies[1 + r].wait())
    line = lax.broadcasted_iota(jnp.int32, (16, B), 0)
    for message, ref in ((R1, r1), (L1, l1)):
        fill(message, ref, yw, None)
        tile = jnp.zeros((16, B), F32)
        for i, (name, r, c) in enumerate(message):
            k = keep(pattern, name[1], r, c)
            tile = jnp.where(line == i, 1.0 if k is True else jnp.where(k, 1.0, 0.0), tile)
        ref[pl.ds(len(message) * B, 16), :] = tile.astype(BF)
    for copy in copies[5:]:
        copy.wait()


def second_kernel(pattern, yw, zin, r2, r3, l3, zz, zw):
    place = lax.rem(lax.axis_index("col"), RING)
    widen(pattern, zw, zin, lambda r: None)
    for message, ref in ((R2, r2), (R3, r3), (L3, l3)):
        fill(message, ref, yw, zw)

    @pl.when(place == 0)
    def _():
        fill(L3, zz, yw, zw)

    @pl.when(place == RING - 1)
    def _():
        fill(R3, zz, yw, zw)


def middle_kernel(pattern, yw, zw, r1, l1, td, e, l, yu, yl, acc):
    clear(yu, 0, UPPER)
    clear(yl, 0, LOWER)
    unpack(R1, r1, {"yU": (yu, 0)})
    unpack(L1, l1, {"yL": (yl, 0)})
    product(
        acc,
        "D",
        (side(zw, "L"), side(yu, "U", 0)),
        (side(zw, "D"), side(yw, "D")),
        (side(zw, "U"), side(yl, "L", 0)),
    )
    eye = jnp.where(
        lax.broadcasted_iota(jnp.int32, (B, B), 0) == lax.broadcasted_iota(jnp.int32, (B, B), 1), 1.5, 0.0
    )
    for r, c in FULL:
        block = -0.5 * acc[rows(r), rows(c)]
        if r == c:
            block = block + eye
        td[rows(r), rows(c)] = masked(keep(pattern, "D", r, c), block).astype(BF)
    for part, left, out in (("L", yl, e), ("U", yu, l)):
        product(acc, part, (side(left, part, 0), side(td, "D", 0)))
        for i, (r, c) in enumerate(BLOCKS[part]):
            out[rows(i), :] = acc[rows(r), rows(c)].astype(BF)
    for i, (name, r, c) in enumerate(L2):
        if name != "sum":
            wide = yw if name[0] == "y" else zw
            l[rows(i), :] = wide[rows(r), pl.ds(COLUMN[name[1]] + c * B, B)]


def relay_kernel(zz, after, r3, l3, r3_out, l3_out):
    place = lax.rem(lax.axis_index("col"), RING)

    @pl.when(place == RING - 1)
    def _():
        r3_out[...] = zz[pl.ds(0, len(R3) * B), :]

    @pl.when(place != RING - 1)
    def _():
        r3_out[...] = r3[...]

    @pl.when(place == 0)
    def _():
        l3_out[...] = zz[pl.ds(0, len(L3) * B), :]

    @pl.when(place != 0)
    def _():
        l3_out[...] = l3[...]


def own_kernel(pattern, yw, zw, td, r2, tl, *rest):
    *sums, ya, acc = rest
    unpack(R2, r2, {"yD": (ya, 0), "zU": None})
    clear(tl, 0, LOWER)
    y_d, z_d, t_d = side(yw, "D"), side(zw, "D"), side(td, "D", 0)
    product(acc, "L", (side(zw, "L"), side(ya, "D", 0)), (z_d, side(yw, "L")))
    for r, c in LOWER:
        tl[rows(r), rows(c)] = masked(keep(pattern, "L", r, c), -0.5 * acc[rows(r), rows(c)]).astype(BF)
    zl, zd, zu, yl, yd, zy = sums
    product(zl, "L", (t_d, side(zw, "L")))
    product(zd, "D", (t_d, z_d))
    product(zu, "U", (t_d, side(zw, "U")))
    product(yl, "L", (y_d, side(tl, "L", 0)))
    product(yd, "D", (y_d, t_d))
    product(zy, "U", (z_d, side(yw, "U")))


def finish(pattern, out, total, part, extra=None):
    for i, (r, c) in enumerate(BLOCKS[part]):
        block = total[rows(r), rows(c)]
        if extra is not None:
            block = block + extra[rows(i), :].astype(F32)
        out[i] = masked(keep(pattern, part, r, c), block.astype(BF))


def late_kernel(pattern, yw, zw, zy, yl, e, l2, tu, yl_out, yu_out, yc, acc):
    unpack(L2, l2, {"yD": (yc, 0), "zL": None, "sum": None})
    clear(yc, 0, [(r, c) for r in range(3) for c in range(3)])
    clear(tu, 0, UPPER)
    finish(pattern, yl_out, yl, "L", e)
    product(acc, "U", (side(zw, "U"), side(yc, "D", 0)), base=zy)
    for r, c in UPPER:
        tu[rows(r), rows(c)] = masked(keep(pattern, "U", r, c), -0.5 * acc[rows(r), rows(c)]).astype(BF)
    product(acc, "U", (side(yw, "D"), side(tu, "U", 0)))
    finish(pattern, yu_out, acc, "U", l2)


def right_kernel(pattern, yw, tu, zd, zu, yd, l1, l2, l3, zu_out, zd_out, yd_out, yl, zl_c, zd_c, tlc, acc):
    clear(yl, 0, LOWER)
    clear(zl_c, 0, L_TOP)
    clear(zd_c, 0, FULL[:12])
    for message, ref in ((L1, l1), (L2, l2), (L3, l3)):
        unpack(message, ref, {"yL": (yl, 0), "yD": None, "zL": (zl_c, 0), "zD": (zd_c, 0), "sum": None})
    clear(tlc, 0, L_TOP)
    mask = l1[pl.ds(len(L1) * B, 16), :].astype(F32)
    product(acc, "L", (side(zl_c, "L", 0), side(yw, "D")), (side(zd_c, "D", 0), side(yl, "L", 0)))
    for i, (r, c) in enumerate(LOWER):
        if r < 3:
            tlc[rows(r), rows(c)] = (-0.5 * acc[rows(r), rows(c)] * mask[i : i + 1, :]).astype(BF)
    t_u = side(tu, "U", 0)
    product(acc, "U", (t_u, side(zd_c, "D", 0)), base=zu)
    finish(pattern, zu_out, acc, "U")
    product(zd_out, "D", (t_u, side(zl_c, "L", 0)), base=zd)
    product(yd_out, "D", (side(yw, "U"), side(tlc, "L", 0)), base=yd)


def last_kernel(pattern, yw, tl, zl, zd, zu, yl, yd, yu, r1, r2, r3, yout, zout, *scratch):
    yu_a, zu_a, zd_a, tua, acc, y_d, z_d, z_l, sems = scratch
    copies = []

    def write(source, target, part):
        at = 0
        for r in range(4):
            size, d = {"L": (4 - r, 0), "D": (4, 4 - r), "U": (r, 8 - r)}[part]
            if size:
                copies.append(
                    pltpu.make_async_copy(
                        source.at[pl.ds(at, size)], target.at[r, pl.ds(d, size)], sems.at[len(copies)]
                    )
                )
                copies[-1].start()
            at += size

    write(zu, zout, "U")
    write(yl, yout, "L")
    write(yu, yout, "U")
    clear(yu_a, 0, UPPER)
    clear(zu_a, 0, UPPER)
    for message, ref in ((R1, r1), (R2, r2), (R3, r3)):
        unpack(message, ref, {"yD": None, "yU": (yu_a, 0), "zD": (zd_a, 0), "zU": (zu_a, 0)})
    clear(tua, 0, UPPER)
    mask = r1[pl.ds(len(R1) * B, 16), :].astype(F32)
    t_l = side(tl, "L", 0)
    product(acc, "D", (t_l, side(zu_a, "U", 0)), base=zd)
    finish(pattern, z_d, acc, "D")
    write(z_d, zout, "D")
    product(acc, "U", (side(zd_a, "D", 0), side(yu_a, "U", 0)), (side(zu_a, "U", 0), side(yw, "D")))
    for i, (r, c) in enumerate(UPPER):
        tua[rows(r), rows(c)] = (-0.5 * acc[rows(r), rows(c)] * mask[i : i + 1, :]).astype(BF)
    product(acc, "D", (side(yw, "L"), side(tua, "U", 0)), base=yd)
    finish(pattern, y_d, acc, "D")
    write(y_d, yout, "D")
    product(acc, "L", (t_l, side(zd_a, "D", 0)), base=zl)
    finish(pattern, z_l, acc, "L")
    write(z_l, zout, "L")
    for copy in copies:
        copy.wait()


VMEM = pl.BlockSpec(memory_space=pltpu.VMEM)
SMEM = pl.BlockSpec(memory_space=pltpu.SMEM)
ANY = pl.BlockSpec(memory_space=pl.ANY)
HBM = pl.BlockSpec(memory_space=pltpu.HBM)


def packed(blocks, masks=False):
    return jax.ShapeDtypeStruct((len(blocks) * B + 16 * masks, B), BF)


def call(kernel, outs, out_specs, ins, scratch, flops, operands, **options):
    outs = tuple(outs)
    moved = sum(v.size * v.dtype.itemsize for v in (*outs, *operands))
    return pl.pallas_call(
        kernel,
        out_shape=outs,
        in_specs=ins,
        out_specs=tuple(out_specs),
        scratch_shapes=scratch,
        compiler_params=pltpu.CompilerParams(vmem_limit_bytes=VMEM_LIMIT),
        cost_estimate=pl.CostEstimate(flops=flops, bytes_accessed=moved, transcendentals=0),
        **options,
    )(*operands)


VMEM_LIMIT = 24 * 2**20
OWN_COST, LATE_COST, RIGHT_COST = 10, 35, 5


def local(ymatrix, zmatrix, pattern):
    count = lax.axis_size("row") * lax.axis_size("col")
    right = [(i, (i + 1) % count) for i in range(count)]
    left = [(b, a) for a, b in right]
    ends = [(i, (i + RING) % count) for i in range(count) if i % RING == RING - 1]
    ends += [((i + RING) % count, i) for i in range(count) if i % RING == 0]
    right_y = [(i, i + 1 if i % RING < RING - 1 else i - RING + 1) for i in range(count)]
    left_y = [(b, a) for a, b in right_y]

    def send(x, pairs):
        return lax.ppermute(x, AXES, pairs)

    wide = jax.ShapeDtypeStruct((S, 3 * S), BF)
    band = jax.ShapeDtypeStruct(ymatrix.shape, BF)
    r1, l1, yw, zin = call(
        first_kernel,
        (packed(R1, True), packed(L1, True), wide, band),
        [VMEM] * 4,
        [HBM] * 3,
        [
            pltpu.VMEM(ymatrix.shape, BF),
            pltpu.SMEM(pattern.shape, jnp.int32),
            pltpu.SemaphoreType.DMA((9,)),
        ],
        0,
        tuple(pltpu.with_memory_space_constraint(v, pltpu.HBM) for v in (pattern, ymatrix, zmatrix)),
    )
    r2, r3, l3, zz, zw = call(
        second_kernel,
        tuple(packed(m) for m in (R2, R3, L3, max(R3, L3, key=len))) + (wide,),
        [VMEM] * 5,
        [SMEM, VMEM, VMEM],
        [],
        0,
        (pattern, yw, zin),
    )
    r1, l1 = send(r1, right), send(l1, left)
    zz = send(zz, ends)
    r2 = send(r2, right)
    td, e, l2 = call(
        middle_kernel,
        (jax.ShapeDtypeStruct((S, S), BF), packed(LOWER), packed(L2)),
        [VMEM] * 3,
        [SMEM] + [VMEM] * 4,
        [pltpu.VMEM((S, S), BF), pltpu.VMEM((S, S), BF), pltpu.VMEM((S, S), F32)],
        6 * S**3,
        (pattern, yw, zw, r1, l1),
    )
    e, l2 = send(e, right), send(l2, left)
    r3, l3 = call(
        relay_kernel,
        (packed(R3), packed(L3)),
        [VMEM] * 2,
        [VMEM, ANY, VMEM, VMEM],
        [],
        0,
        (zz, td, r3, l3),
    )
    r3, l3 = send(r3, right_y), send(l3, left_y)
    square, total = jax.ShapeDtypeStruct((S, S), BF), jax.ShapeDtypeStruct((S, S), F32)
    one, half = pltpu.VMEM((S, S), BF), pltpu.VMEM((S, 2 * S), BF)
    full = pltpu.VMEM((S, S), F32)
    tl, zl, zd, zu, yl, yd, zy = call(
        own_kernel,
        (square,) + (total,) * 6,
        [VMEM] * 7,
        [SMEM] + [VMEM] * 4,
        [one, full],
        OWN_COST * S**3,
        (pattern, yw, zw, td, r2),
    )
    lower, upper = (jax.ShapeDtypeStruct((len(v), B, B), BF) for v in (LOWER, UPPER))
    tu, yl, yu = call(
        late_kernel,
        (square, lower, upper),
        [VMEM] * 3,
        [SMEM] + [VMEM] * 6,
        [one, full],
        LATE_COST * S**3,
        (pattern, yw, zw, zy, yl, e, l2),
    )
    zu, zd, yd = call(
        right_kernel,
        (upper, total, total),
        [VMEM] * 3,
        [SMEM] + [VMEM] * 8,
        [one, one, one, one, full],
        RIGHT_COST * S**3,
        (pattern, yw, tu, zd, zu, yd, l1, l2, l3),
        input_output_aliases={3: 1, 5: 2},
    )
    whole = jax.ShapeDtypeStruct(ymatrix.shape, BF)
    return call(
        last_kernel,
        (whole, whole),
        [ANY] * 2,
        [SMEM] + [VMEM] * 11,
        [
            one,
            one,
            one,
            one,
            full,
            pltpu.VMEM((16, B, B), BF),
            pltpu.VMEM((16, B, B), BF),
            pltpu.VMEM((10, B, B), BF),
            pltpu.SemaphoreType.DMA((22,)),
        ],
        10 * S**3,
        (pattern, yw, tl, zl, zd, zu, yl, yd, yu, r1, r2, r3),
    )


def solution(mesh):
    band = P(AXES, None, None, None)
    return jax.shard_map(
        local,
        mesh=mesh,
        in_specs=(band, band, P(AXES, None)),
        out_specs=(band, band),
        check_vma=False,
    )
```
